32 devices in a mesh: groups: 2 (over x), blk: 16 (over z, y, core).
Axes of the slice: x: 2, y: 2, z: 4, core: 2. Of those that a mesh axis runs over, the one named last changes fastest.
Arguments:
- image_feats: bfloat16 [4096, 768], P(('groups', 'blk')), parts along dimension 0, may hold values from -32 to 32
- text_feats: bfloat16 [4096, 512], P(('groups', 'blk')), parts along dimension 0, may hold values from -32 to 32
- class_ids: int32 [4096], P(('groups', 'blk')), parts along dimension 0, may hold values from 0 to 2047
- w_img: bfloat16 [768, 512], replicated, may hold values from -1 to 1
- w_txt: bfloat16 [512, 512], replicated, may hold values from -1 to 1
Outputs:
- loss: float32 [2], P('groups'), parts along dimension 0
- grad_w_img: float32 [1536, 512], P('groups'), parts along dimension 0
- grad_w_txt: float32 [1024, 512], P('groups'), parts along dimension 0
The draws below stay inside these ranges and needn't reach their ends.
There are 2 independent parts, one for each index of `groups`. The reference program is written for one: setup_inputs(seed, part) draws one part's arguments, and reference() takes and returns one part's arrays. A program takes and returns all parts, laid end to end along the dimension named above; an argument that names none is the same for every part. Nothing has to cross between parts.
All inputs are finite; a program needn't handle non-finite values.
Results may differ from the reference program's by a relative error of at most 0.0021.
Values may be sent and summed in bfloat16 or wider, within the bound.
A program may use at most 64 MiB of HBM per device.

```python
import math
import jax
import jax.numpy as jnp
import numpy as np
from jax import lax

DI = 768
DT = 512
E = 512
ROWS = 128
TOKENS = 2048


primary_count = 4


global_count = 16


def shared_weight(key):
    key = jax.random.fold_in(key, 5)
    return jnp.clip(jax.random.normal(key, (DT, E), jnp.float32), -5.0, 5.0)


def draw_w_txt(key, part):
    shared = shared_weight(key)
    key = jax.random.fold_in(key, 11)
    jitter = jax.random.normal(key, (DT, E), jnp.float32)
    return jnp.clip((shared + 0.3 * jitter) * DT ** (-0.5), -1.0, 1.0).astype(jnp.bfloat16)


def draw_w_img(key, part):
    shared = shared_weight(key)
    key = jax.random.fold_in(key, 12)
    first_key, second_key = jax.random.split(key)
    upper = shared + 0.5 * jax.random.normal(first_key, (DT, E), jnp.float32)
    remainder = jax.random.normal(second_key, (DI - DT, E), jnp.float32)
    whole = jnp.concatenate([upper, remainder], axis=0)
    return jnp.clip(whole * DI ** (-0.5), -1.0, 1.0).astype(jnp.bfloat16)


def latent_rows(key):
    key = jax.random.fold_in(key, 6)
    subkeys = jax.random.split(key, 6)
    block_count = TOKENS // ROWS
    block_dirs = jax.random.normal(subkeys[0], (block_count * primary_count, DT), jnp.float32)
    global_dirs = jax.random.normal(subkeys[1], (global_count, DT), jnp.float32)
    primary = jax.random.randint(subkeys[2], (TOKENS,), 0, primary_count)
    chosen = jax.random.randint(subkeys[3], (TOKENS,), 0, global_count)
    row_block = jnp.arange(TOKENS, dtype=jnp.int32) // ROWS
    jitter = jax.random.normal(subkeys[5], (TOKENS, DT), jnp.float32)
    picked = block_dirs[row_block * primary_count + primary]
    return picked + 0.6 * global_dirs[chosen] + 0.7 * jitter


def draw_image_feats(key, part):
    widest = 2.0
    latent = latent_rows(key)
    key = jax.random.fold_in(key, 21)
    first_key, second_key = jax.random.split(key)
    remainder = 0.5 * jax.random.normal(first_key, (TOKENS, DI - DT), jnp.float32)
    row_scale = jnp.exp(jax.random.uniform(second_key, (TOKENS, 1), jnp.float32, 0.0, math.log(widest)))
    whole = jnp.concatenate([latent, remainder], axis=1) * row_scale
    return jnp.clip(whole, -32.0, 32.0).astype(jnp.bfloat16)


def draw_text_feats(key, part):
    widest = 2.0
    latent = latent_rows(key)
    key = jax.random.fold_in(key, 22)
    first_key, second_key = jax.random.split(key)
    jitter = 0.5 * jax.random.normal(first_key, (TOKENS, DT), jnp.float32)
    row_scale = jnp.exp(jax.random.uniform(second_key, (TOKENS, 1), jnp.float32, 0.0, math.log(widest)))
    whole = (latent + jitter) * row_scale
    return jnp.clip(whole, -32.0, 32.0).astype(jnp.bfloat16)


def touch_ends(array, stream_key, least, largest):
    place = [jax.random.randint(jax.random.fold_in(stream_key, axis), (), 0, length) for axis, length in enumerate(array.shape)]
    main_axis = array.shape.index(max(array.shape))
    beside = place[:main_axis] + [(place[main_axis] + 1) % array.shape[main_axis]] + place[main_axis + 1:]
    return array.at[tuple(place)].set(least).at[tuple(beside)].set(largest)


def rank_bounds(amount, skew):
    loads = [(1 << 20) // math.isqrt(grade ** skew) + 1 for grade in range(1, amount + 1)]
    width = 1 + sum(loads) // (1 << 30)
    return np.cumsum(np.array([max(1, weight // width) for weight in loads]))


def skewed_ids(key, extent, amount, skew):
    listing = rank_bounds(amount, skew)
    pick = jax.random.randint(jax.random.fold_in(key, 1), extent, 0, int(listing[amount - 1]))
    grade = jnp.searchsorted(jnp.asarray(listing, jnp.int32), pick, side="right")
    return jax.random.permutation(jax.random.fold_in(key, 2), amount)[grade].astype(jnp.int32)


def setup_inputs(seed: int = 0, part: int = 0) -> dict:
    arg_keys = jax.random.split(jax.random.key(seed), 6)
    part_keys = jax.random.split(jax.random.fold_in(arg_keys[5], part), 6)
    return {
        "image_feats": draw_image_feats(jax.random.fold_in(jax.random.fold_in(arg_keys[5], part), 71), part),
        "text_feats": draw_text_feats(jax.random.fold_in(jax.random.fold_in(arg_keys[5], part), 71), part),
        "class_ids": touch_ends(skewed_ids(part_keys[2], (TOKENS,), TOKENS, 1), jax.random.fold_in(part_keys[2], 3), 0, TOKENS - 1).astype(jnp.int32),
        "w_img": draw_w_img(jax.random.fold_in(arg_keys[5], 71), part),
        "w_txt": draw_w_txt(jax.random.fold_in(arg_keys[5], 71), part),
    }


LOGIT_SCALE = 10.0
LOGIT_BIAS = -10.0
NORM_EPS = 1e-06

def reference(image_feats, text_feats, class_ids, w_img, w_txt):
    exact = lax.Precision.HIGHEST
    proj_img = jnp.dot(image_feats, w_img, preferred_element_type=jnp.float32)
    inv_img = lax.rsqrt(lax.optimization_barrier(jnp.sum(proj_img * proj_img, axis=1, keepdims=True)) + NORM_EPS)
    unit_img = proj_img * inv_img
    proj_txt = jnp.dot(text_feats, w_txt, preferred_element_type=jnp.float32)
    inv_txt = lax.rsqrt(lax.optimization_barrier(jnp.sum(proj_txt * proj_txt, axis=1, keepdims=True)) + NORM_EPS)
    scaled_txt = (text_feats.astype(jnp.float32) * inv_txt).astype(jnp.bfloat16)
    unit_txt = jnp.dot(scaled_txt, w_txt, preferred_element_type=jnp.float32)
    txt_weight = w_txt.astype(jnp.float32)
    query = jnp.dot(unit_img, txt_weight.T, precision=exact).astype(jnp.bfloat16)
    span_rows = 4 * ROWS
    span_count = TOKENS // span_rows

    def block_step(state_now, block_index):
        loss_sum, dot_sum = state_now
        offset = (block_index * span_rows).astype(jnp.int32)
        query_rows = lax.dynamic_slice_in_dim(query, offset, span_rows, 0)
        block_ids = lax.dynamic_slice_in_dim(class_ids, offset, span_rows, 0)
        cosine = jnp.dot(query_rows, scaled_txt.T, preferred_element_type=jnp.float32)
        logits = LOGIT_SCALE * cosine + LOGIT_BIAS
        labels = jnp.where(block_ids[:, None] == class_ids[None, :], 1.0, -1.0).astype(cosine.dtype)
        loss_sum = loss_sum + jnp.sum(jax.nn.softplus(-labels * logits))
        slope = -LOGIT_SCALE * labels * jax.nn.sigmoid(-labels * logits) / TOKENS
        slope_b = slope.astype(jnp.bfloat16)
        across = jnp.dot(slope_b, scaled_txt, preferred_element_type=jnp.float32)
        back = jnp.dot(scaled_txt.T, slope_b.T, preferred_element_type=jnp.float32)
        dot_sum = dot_sum + lax.optimization_barrier(jnp.sum(slope * cosine, axis=0))
        return ((loss_sum, dot_sum), (across, back))
    start_carry = (jnp.zeros((), jnp.float32), jnp.zeros((TOKENS,), jnp.float32))
    (loss_sum, row_dot), (across_blocks, back_blocks) = lax.scan(block_step, start_carry, jnp.arange(span_count, dtype=jnp.int32))
    across = across_blocks.reshape(TOKENS, DT)
    back = jnp.concatenate([back_blocks[index] for index in range(span_count)], axis=1)
    d_unit_img = jnp.dot(across, txt_weight, precision=exact)
    d_proj_img = inv_img * (d_unit_img - unit_img * lax.optimization_barrier(jnp.sum(unit_img * d_unit_img, axis=1, keepdims=True)))
    grad_w_img = jnp.dot(image_feats.astype(jnp.float32).T, d_proj_img, precision=exact)
    text_first = jnp.dot(back, unit_img, precision=exact)
    text_second = jnp.dot(scaled_txt.astype(jnp.float32).T, unit_txt * row_dot[:, None], precision=exact)
    grad_w_txt = text_first - text_second
    loss = (loss_sum / TOKENS).reshape(1)
    return (loss, grad_w_img, grad_w_txt)
```

```python
import functools

import jax
import jax.numpy as jnp
from jax import lax
from jax.experimental import pallas as pl
from jax.experimental.pallas import tpu as pltpu
from jax.sharding import PartitionSpec as P

LOGIT_SCALE = 10.0
LOGIT_BIAS = -10.0
NORM_EPS = 1e-06
F32 = jnp.float32
BF16 = jnp.bfloat16
LEVELS = 32767.0


def grid_of(n):
    chips = n // 2
    fast = 1
    while fast * fast * 4 <= chips and chips % (fast * 2) == 0:
        fast *= 2
    return chips // fast, fast


def chunk_rows(rows, n):
    slow, fast = grid_of(n)
    part = rows // (2 * fast)
    return part, -(-part // (slow * 16)) * 16


def split(value):
    high = value.astype(BF16)
    return high, (value - high.astype(F32)).astype(BF16)


def quantize(value):
    peak = jnp.maximum(jnp.max(jnp.abs(value), axis=0, keepdims=True), 1e-30)
    return jnp.round(value * (LEVELS / peak)).astype(jnp.int32).astype(jnp.int16), peak / LEVELS


def dequantize(value, scale):
    return value.astype(jnp.int32).astype(F32) * scale


def dot_nn(a, b):
    return jnp.dot(a, b, preferred_element_type=F32)


def dot_nt(a, b):
    return lax.dot_general(a, b, (((1,), (1,)), ((), ())), preferred_element_type=F32)


def dot_tn(a, b):
    return lax.dot_general(a, b, (((0,), (0,)), ((), ())), preferred_element_type=F32)


def as_column(row):
    length = row.shape[1]
    return jnp.broadcast_to(row, (length, length)).T[:, :1]


def kernel(
    n,
    img_ref, txt_ref, ids_ref, w_img_ref, w_txt_ref,
    loss_ref, full_ref, scale_ref,
    rows_all, ids_all, message, arrived, across_ref, loss_acc, grads,
    out_core, in_core, out_fast, in_fast, own_part, out_slow, in_slow,
    out_core_scale, in_core_scale, out_fast_scale, in_fast_scale, out_slow_scale, in_slow_scale,
    rows_send, rows_recv, ids_sem, msg_sem, core_sem, fast_sem, slow_sem, full_send, full_recv,
    scale_sem,
):
    slow, fast = grid_of(n)
    chunk = full_ref.shape[1]
    part = (img_ref.shape[1] + txt_ref.shape[1]) // (2 * fast)
    own = img_ref.shape[0]
    total_rows = n * own
    me = lax.axis_index("blk")
    mc = lax.rem(me, 2)
    my = lax.rem(me // 2, fast)
    mz = me // (2 * fast)

    def device(z, y, c):
        return (z * fast + y) * 2 + c

    sibling = device(mz, my, 1 - mc)

    barrier = pltpu.get_barrier_semaphore()

    def greet(i, carry):
        pl.semaphore_signal(barrier, inc=1, device_id={"blk": lax.rem(me + i, n)})
        return carry

    lax.fori_loop(1, n, greet, 0)

    proj_txt = dot_nn(txt_ref[...], w_txt_ref[...])
    inv_txt = lax.rsqrt(jnp.sum(proj_txt * proj_txt, axis=1, keepdims=True) + NORM_EPS)
    rows_all[me] = (txt_ref[...].astype(F32) * inv_txt).astype(BF16)
    ids_all[me] = ids_ref[...]

    pl.semaphore_wait(barrier, n - 1)

    def spread(buffer, slot, send_sem, recv_sem, use):
        def copy(z, y, c, dst, k):
            return pltpu.make_async_remote_copy(
                src_ref=buffer.at[slot(z, y, c)],
                dst_ref=buffer.at[slot(z, y, c)],
                send_sem=send_sem.at[k],
                recv_sem=recv_sem.at[device(z, y, c)],
                device_id={"blk": dst},
            )

        base = slow - 1
        last = base + slow * (fast - 1)

        for dy in range(1, fast):
            copy(mz, my, mc, device(mz, lax.rem(my + dy, fast), mc), base + dy - 1).start()
        for dz in range(1, slow):
            copy(mz, my, mc, device(lax.rem(mz + dz, slow), my, mc), dz - 1).start()
        copy(mz, my, mc, sibling, last).start()

        def step(t, carry):
            dz, dy = t // fast, lax.rem(t, fast)
            z, y = lax.rem(mz + dz, slow), lax.rem(my + dy, fast)

            @pl.when(t > 0)
            def _():
                copy(z, y, mc, sibling, last + t).wait_recv()

                @pl.when(dy == 0)
                def _():
                    for other in range(1, fast):
                        k = base + dz * (fast - 1) + other - 1
                        copy(z, y, mc, device(mz, lax.rem(my + other, fast), mc), k).start()

                copy(z, y, mc, sibling, last + t).start()

            copy(z, y, 1 - mc, sibling, 0).wait_recv()
            use(z * fast + y)
            return carry

        lax.fori_loop(0, slow * fast, step, 0)

        def drain(k, carry):
            copy(mz, my, mc, sibling, k).wait_send()
            return carry

        return lambda: lax.fori_loop(0, n - 1, drain, 0)

    def ids_copy(i):
        return pltpu.make_async_remote_copy(
            src_ref=ids_all.at[me],
            dst_ref=ids_all.at[me],
            send_sem=ids_sem.at[0],
            recv_sem=ids_sem.at[1],
            device_id={"blk": lax.rem(me + i, n)},
        )

    def ids_start(i, carry):
        ids_copy(i).start()
        return carry

    lax.fori_loop(1, n, ids_start, 0)
    ids_whole = pltpu.make_async_remote_copy(
        src_ref=ids_all.at[pl.ds(0, n - 1)],
        dst_ref=ids_all.at[pl.ds(0, n - 1)],
        send_sem=ids_sem.at[0],
        recv_sem=ids_sem.at[1],
        device_id={"blk": sibling},
    )

    proj_img = dot_nn(img_ref[...], w_img_ref[...])
    inv_img = lax.rsqrt(jnp.sum(proj_img * proj_img, axis=1, keepdims=True) + NORM_EPS)
    unit_img = proj_img * inv_img
    unit_high, unit_low = split(unit_img)
    query = (dot_nt(unit_high, w_txt_ref[...]) + dot_nt(unit_low, w_txt_ref[...])).astype(BF16)
    unit_txt = dot_nn(rows_all[me], w_txt_ref[...])
    own_ids = as_column(ids_ref[...].astype(F32))

    across_ref[...] = jnp.zeros_like(across_ref)
    loss_acc[...] = jnp.zeros_like(loss_acc)

    def visit(chip):
        @pl.when(chip == me // 2)
        def _():
            ids_whole.wait()

        block = rows_all[pl.ds(2 * chip, 2)].reshape(2 * own, rows_all.shape[2])
        ids = jnp.concatenate([ids_all[2 * chip], ids_all[2 * chip + 1]], axis=1).astype(F32)
        cosine = dot_nt(query, block)
        logits = LOGIT_SCALE * cosine + LOGIT_BIAS
        labels = jnp.where(own_ids == ids, 1.0, -1.0).astype(F32)
        margin = -labels * logits
        decay = jnp.exp(-jnp.abs(margin))
        loss_acc[...] += jnp.sum(jnp.maximum(margin, 0.0) + jnp.log1p(decay), axis=0, keepdims=True)
        gate = jnp.where(margin >= 0.0, 1.0, decay) / (1.0 + decay)
        slope = (-LOGIT_SCALE / total_rows) * labels * gate
        across_ref[...] += dot_nn(slope.astype(BF16), block)
        dots = jnp.sum(slope * cosine, axis=0, keepdims=True)
        message[2 * chip, :, pl.ds(0, own)] = dots[:, :own]
        message[2 * chip + 1, :, pl.ds(0, own)] = dots[:, own:]

    rows_done = spread(rows_all, device, rows_send, rows_recv, visit)

    losses = loss_acc[:, :own] + loss_acc[:, own:]
    message[:, :, pl.ds(own, own)] = jnp.broadcast_to(losses[None], (n, 1, own))
    arrived[me] = message[me]

    def msg_start(i, carry):
        dst = lax.rem(me + i, n)
        pltpu.make_async_remote_copy(
            src_ref=message.at[dst],
            dst_ref=arrived.at[me],
            send_sem=msg_sem.at[0],
            recv_sem=msg_sem.at[1],
            device_id={"blk": dst},
        ).start()
        return carry

    lax.fori_loop(1, n, msg_start, 0)

    def keep(first, value):
        done = 0
        while done < value.shape[0]:
            index, offset = divmod(first + done, part)
            count = min(part - offset, value.shape[0] - done)
            grads[index, pl.ds(offset, count)] = value[done:done + count]
            done += count

    across = across_ref[...]
    across_high, across_low = split(across)
    d_unit_img = dot_nn(across_high, w_txt_ref[...]) + dot_nn(across_low, w_txt_ref[...])
    d_proj_img = inv_img * (
        d_unit_img - unit_img * jnp.sum(unit_img * d_unit_img, axis=1, keepdims=True)
    )
    d_high, d_low = split(d_proj_img)
    img = img_ref[...]
    if slow * chunk > part:
        grads[:, pl.ds(part, slow * chunk - part)] = jnp.zeros(
            (2 * fast, slow * chunk - part, grads.shape[2]), F32
        )
    keep(0, dot_tn(jnp.concatenate([img, img]), jnp.concatenate([d_high, d_low])))

    text_first = dot_tn(
        jnp.concatenate([across_high, across_low, across_high]),
        jnp.concatenate([unit_high, unit_high, unit_low]),
    )
    pltpu.make_async_remote_copy(
        src_ref=message.at[pl.ds(0, n - 1)],
        dst_ref=arrived.at[pl.ds(0, n - 1)],
        send_sem=msg_sem.at[0],
        recv_sem=msg_sem.at[1],
        device_id={"blk": sibling},
    ).wait()
    everything = jnp.sum(arrived[...], axis=0)
    loss_ref[...] = jnp.sum(everything[:, own:], axis=1, keepdims=True) / total_rows
    row_dot = as_column(everything[:, :own])
    text_high, text_low = split(unit_txt * row_dot)
    rows_own = rows_all[me]
    text_second = dot_tn(
        jnp.concatenate([rows_own, rows_own]), jnp.concatenate([text_high, text_low])
    )
    keep(img_ref.shape[1], text_first - text_second)

    class Message:
        def __init__(self, source, target, source_scale, target_scale, sem, index, dst):
            self.source, self.source_scale, self.index = source, source_scale, index
            self.target, self.target_scale = target, target_scale
            self.copies = [
                pltpu.make_async_remote_copy(
                    src_ref=a.at[index],
                    dst_ref=b.at[index],
                    send_sem=sem.at[2 * k, index],
                    recv_sem=sem.at[2 * k + 1, index],
                    device_id={"blk": dst},
                )
                for k, (a, b) in enumerate([(source, target), (source_scale, target_scale)])
            ]

        def send(self, value):
            self.source[self.index], self.source_scale[self.index] = quantize(value)
            for copy in self.copies:
                copy.start()

        def receive(self):
            for copy in self.copies:
                copy.wait_recv()
            return dequantize(self.target[self.index], self.target_scale[self.index])

        def finish(self):
            for copy in self.copies:
                copy.wait_send()

    def core_message(j):
        return Message(out_core, in_core, out_core_scale, in_core_scale, core_sem, j, sibling)

    def fast_message(d):
        dst = device(mz, lax.rem(my + d, fast), mc)
        return Message(out_fast, in_fast, out_fast_scale, in_fast_scale, fast_sem, d - 1, dst)

    def slow_message(d):
        dst = device(lax.rem(mz + d, slow), my, mc)
        return Message(out_slow, in_slow, out_slow_scale, in_slow_scale, slow_sem, d - 1, dst)

    for d in list(range(1, fast)) + [0]:
        j = lax.rem(my + d, fast)
        core_message(j).send(grads[(1 - mc) * fast + j])
    for d in range(1, fast):
        j = lax.rem(my + d, fast)
        fast_message(d).send(grads[mc * fast + j] + core_message(j).receive())
    part_sum = grads[mc * fast + my] + core_message(my).receive()
    for d in range(1, fast):
        part_sum = part_sum + fast_message(d).receive()
    own_part[...] = part_sum.reshape(own_part.shape)
    for d in range(1, slow):
        slow_message(d).send(own_part[lax.rem(mz + d, slow)])
    chunk_sum = own_part[mz]
    for d in range(1, slow):
        chunk_sum = chunk_sum + slow_message(d).receive()

    def place(z, y, c):
        return (c * fast + y) * slow + z

    mine = place(mz, my, mc)
    full_ref[mine], scale_ref[mine] = quantize(chunk_sum)

    def scale_start(i, carry):
        pltpu.make_async_remote_copy(
            src_ref=scale_ref.at[mine],
            dst_ref=scale_ref.at[mine],
            send_sem=scale_sem.at[0],
            recv_sem=scale_sem.at[1],
            device_id={"blk": lax.rem(me + i, n)},
        ).start()
        return carry

    lax.fori_loop(1, n, scale_start, 0)
    full_done = spread(full_ref, place, full_send, full_recv, lambda chip: None)
    pltpu.make_async_remote_copy(
        src_ref=scale_ref.at[pl.ds(0, n - 1)],
        dst_ref=scale_ref.at[pl.ds(0, n - 1)],
        send_sem=scale_sem.at[0],
        recv_sem=scale_sem.at[1],
        device_id={"blk": sibling},
    ).wait()

    rows_done()
    for j in range(fast):
        core_message(j).finish()
    for d in range(1, fast):
        fast_message(d).finish()
    for d in range(1, slow):
        slow_message(d).finish()
    full_done()


def body(n, image_feats, text_feats, class_ids, w_img, w_txt):
    slow, fast = grid_of(n)
    own, wide_img = image_feats.shape
    wide_txt = text_feats.shape[1]
    shared = w_img.shape[1]
    part, chunk = chunk_rows(wide_img + wide_txt, n)
    dma = pltpu.SemaphoreType.DMA
    loss, full, scale = pl.pallas_call(
        functools.partial(kernel, n),
        out_shape=(
            jax.ShapeDtypeStruct((1, 1), F32),
            jax.ShapeDtypeStruct((n, chunk, shared), jnp.int16),
            jax.ShapeDtypeStruct((n, 1, shared), F32),
        ),
        in_specs=[pl.BlockSpec(memory_space=pltpu.VMEM)] * 5,
        out_specs=(pl.BlockSpec(memory_space=pltpu.VMEM),) * 3,
        scratch_shapes=[
            pltpu.VMEM((n, own, wide_txt), BF16),
            pltpu.VMEM((n, 1, own), jnp.int32),
            pltpu.VMEM((n, 1, 2 * own), F32),
            pltpu.VMEM((n, 1, 2 * own), F32),
            pltpu.VMEM((own, wide_txt), F32),
            pltpu.VMEM((1, 2 * own), F32),
            pltpu.VMEM((2 * fast, slow * chunk, shared), F32),
            pltpu.VMEM((fast, slow * chunk, shared), jnp.int16),
            pltpu.VMEM((fast, slow * chunk, shared), jnp.int16),
            pltpu.VMEM((fast - 1, slow * chunk, shared), jnp.int16),
            pltpu.VMEM((fast - 1, slow * chunk, shared), jnp.int16),
            pltpu.VMEM((slow, chunk, shared), F32),
            pltpu.VMEM((slow - 1, chunk, shared), jnp.int16),
            pltpu.VMEM((slow - 1, chunk, shared), jnp.int16),
            pltpu.VMEM((fast, 1, shared), F32),
            pltpu.VMEM((fast, 1, shared), F32),
            pltpu.VMEM((fast - 1, 1, shared), F32),
            pltpu.VMEM((fast - 1, 1, shared), F32),
            pltpu.VMEM((slow - 1, 1, shared), F32),
            pltpu.VMEM((slow - 1, 1, shared), F32),
            dma((n - 1,)),
            dma((n,)),
            dma((2,)),
            dma((2,)),
            dma((4, fast)),
            dma((4, fast - 1)),
            dma((4, slow - 1)),
            dma((n - 1,)),
            dma((n,)),
            dma((2,)),
        ],
        compiler_params=pltpu.CompilerParams(
            collective_id=0, has_side_effects=True, vmem_limit_bytes=48 * 2**20
        ),
    )(image_feats, text_feats, class_ids.reshape(1, own), w_img, w_txt)
    grads = full.astype(F32) * scale
    grads = grads.reshape(2 * fast, slow * chunk, shared)[:, :part].reshape(-1, shared)
    return loss.reshape(1), grads[:wide_img], grads[wide_img:]


def solution(mesh):
    return jax.shard_map(
        functools.partial(body, mesh.shape["blk"]),
        mesh=mesh,
        in_specs=(
            P(("groups", "blk"), None),
            P(("groups", "blk"), None),
            P(("groups", "blk")),
            P(),
            P(),
        ),
        out_specs=(P("groups"), P("groups", None), P("groups", None)),
        check_vma=False,
    )
```

```python
import functools

import jax
import jax.numpy as jnp
from jax import lax
from jax.experimental import pallas as pl
from jax.experimental.pallas import tpu as pltpu
from jax.sharding import PartitionSpec as P

LOGIT_SCALE = 10.0
LOGIT_BIAS = -10.0
NORM_EPS = 1e-06
F32 = jnp.float32
BF16 = jnp.bfloat16
LEVELS = 32767.0


LANES = 128
HEAD = 16
SLOW = 4


def padded(rows):
    return -(-rows // 16) * 16


def split(value):
    high = value.astype(BF16)
    return high, (value - high.astype(F32)).astype(BF16)


def pack(value, rows):
    peak = jnp.maximum(jnp.max(jnp.abs(value), axis=0, keepdims=True), 1e-30)
    power = jnp.ceil(jnp.log2(peak * (1.0001 / LEVELS)))
    levels = jnp.round(value * jnp.exp2(-power))
    parts = [levels]
    if rows > value.shape[0]:
        parts.append(jnp.zeros((rows - value.shape[0], LANES), F32))
    parts.append(jnp.broadcast_to(power, (HEAD, LANES)))
    return jnp.concatenate(parts).astype(jnp.int32).astype(jnp.int16)


def unpack(message, part, rows):
    wide = message.astype(jnp.int32).astype(F32)
    return wide[:part] * jnp.exp2(wide[rows:rows + 1])


def dot_nn(a, b):
    return jnp.dot(a, b, preferred_element_type=F32)


def dot_nt(a, b):
    return lax.dot_general(a, b, (((1,), (1,)), ((), ())), preferred_element_type=F32)


def dot_tn(a, b):
    return lax.dot_general(a, b, (((0,), (0,)), ((), ())), preferred_element_type=F32)


def as_column(row):
    length = row.shape[1]
    return jnp.broadcast_to(row, (length, length)).T[:, :1]


def loop(first, last, use):
    def step(i, carry):
        use(i)
        return carry

    lax.fori_loop(first, last, step, 0)


def kernel(
    n,
    img_hbm, txt_hbm, ids_hbm, w_img_hbm, w_txt_hbm,
    loss_ref, full_ref,
    w_img_ref, w_txt_ref, txt_ref, img_all, txt_all, ids_rows, ids_cols,
    img_turned, across_high, across_low, unit_high, unit_low, inv_all, query, across,
    row_ids, txt_turned, text_high, text_low, dots, loss_acc, loss_slow, loss_plane,
    grads, out_core, in_core, out_fast, in_fast, out_slow, in_slow,
    local_sem, img_send, img_recv, txt_sem, ids_sem, loss_sem,
    core_sem, fast_sem, slow_sem, full_send, full_recv,
):
    fast = n // (2 * SLOW)
    plane = 2 * fast
    own, wide_img = img_all.shape[1:]
    wide_txt = txt_all.shape[2]
    blocks, size = query.shape[:2]
    part = (wide_img + wide_txt) // plane
    rows = full_ref.shape[1] - HEAD
    per = size // own
    total_rows = n * own
    me = lax.axis_index("blk")
    mp = lax.rem(me, plane)
    mc = lax.rem(me, 2)
    my = mp // 2
    mz = me // plane

    def device(z, y, c):
        return (z * fast + y) * 2 + c

    def along(d):
        return device(lax.rem(mz + d, SLOW), my, mc)

    def across_fast(d):
        return device(mz, lax.rem(my + d, fast), mc)

    def in_plane(d):
        return mz * plane + lax.rem(mp + d, plane)

    sibling = device(mz, my, 1 - mc)

    barrier = pltpu.get_barrier_semaphore()
    for d in range(1, SLOW):
        pl.semaphore_signal(barrier, inc=1, device_id={"blk": along(d)})
    loop(1, plane, lambda d: pl.semaphore_signal(barrier, inc=1, device_id={"blk": in_plane(d)}))

    loads = [
        pltpu.make_async_copy(a, b, local_sem.at[k])
        for k, (a, b) in enumerate([
            (txt_hbm, txt_ref), (w_txt_hbm, w_txt_ref), (img_hbm, img_all.at[mp]),
            (w_img_hbm, w_img_ref), (ids_hbm, ids_rows.at[mp]), (ids_hbm, ids_cols.at[mz]),
        ])
    ]
    for load in loads:
        load.start()

    def remote(src, dst, send, recv, where):
        return pltpu.make_async_remote_copy(
            src_ref=src, dst_ref=dst, send_sem=send, recv_sem=recv, device_id={"blk": where}
        )

    def img_copy(y, c, dst, k):
        slot = img_all.at[y * 2 + c]
        return remote(slot, slot, img_send.at[k], img_recv.at[y * 2 + c], dst)

    def txt_copy(z, d):
        return remote(txt_all.at[z], txt_all.at[z], txt_sem.at[0, d], txt_sem.at[1, z], along(d))

    def ids_row_copy(d):
        slot = ids_rows.at[mp]
        return remote(slot, slot, ids_sem.at[0], ids_sem.at[1], in_plane(d))

    def ids_col_copy(d):
        slot = ids_cols.at[mz]
        return remote(slot, slot, ids_sem.at[2], ids_sem.at[3], along(d))

    loads[0].wait()
    loads[1].wait()
    proj_txt = dot_nn(txt_ref[...], w_txt_ref[...])
    inv_txt = lax.rsqrt(jnp.sum(proj_txt * proj_txt, axis=1, keepdims=True) + NORM_EPS)
    txt_all[mz] = (txt_ref[...].astype(F32) * inv_txt).astype(BF16)
    for load in loads[2:]:
        load.wait()
    pl.semaphore_wait(barrier, SLOW + plane - 2)

    for d in range(1, SLOW):
        txt_copy(mz, d).start()
    loop(1, fast, lambda d: img_copy(my, mc, across_fast(d), d).start())
    img_copy(my, mc, sibling, 0).start()
    for d in range(1, SLOW):
        ids_col_copy(d).start()
    loop(1, plane, lambda d: ids_row_copy(d).start())

    loss_acc[...] = jnp.zeros_like(loss_acc)

    def pass_on(d):
        y = lax.rem(my + d, fast)
        img_copy(y, mc, sibling, 0).wait_recv()
        img_copy(y, mc, sibling, fast - 1 + d).start()

    loop(1, fast, pass_on)
    loop(0, fast, lambda d: img_copy(d, 1 - mc, sibling, 0).wait_recv())
    remote(
        ids_rows.at[pl.ds(0, plane - 1)], ids_rows.at[pl.ds(0, plane - 1)],
        ids_sem.at[0], ids_sem.at[1], sibling,
    ).wait()

    def project(block):
        img = img_all[pl.ds(block * per, per)].reshape(size, wide_img)
        proj_img = dot_nn(img, w_img_ref[...])
        inv_img = lax.rsqrt(jnp.sum(proj_img * proj_img, axis=1, keepdims=True) + NORM_EPS)
        unit_img = proj_img * inv_img
        high, low = split(unit_img)
        query[block] = (dot_nt(high, w_txt_ref[...]) + dot_nt(low, w_txt_ref[...])).astype(BF16)
        unit_high[block], unit_low[block] = high, low
        inv_all[block] = inv_img
        img_turned[block] = img.T
        across[block] = jnp.zeros((size, wide_txt), F32)
        row_ids[block] = jnp.concatenate(
            [as_column(ids_rows[block * per + i].astype(F32)) for i in range(per)]
        )

    loop(0, blocks, project)
    remote(
        ids_cols.at[pl.ds(0, SLOW - 1)], ids_cols.at[pl.ds(0, SLOW - 1)],
        ids_sem.at[2], ids_sem.at[3], sibling,
    ).wait()

    def visit(d):
        z = lax.rem(mz + d, SLOW)

        @pl.when(d > 0)
        def _():
            txt_copy(z, 0).wait_recv()

        text = txt_all[z]
        ids = ids_cols[z].astype(F32)
        dots[...] = jnp.zeros_like(dots)

        def tile(block):
            cosine = dot_nt(query[block], text)
            logits = LOGIT_SCALE * cosine + LOGIT_BIAS
            labels = jnp.where(row_ids[block] == ids, 1.0, -1.0).astype(F32)
            margin = -labels * logits
            decay = jnp.exp(-jnp.abs(margin))
            terms = jnp.maximum(margin, 0.0) + jnp.log1p(decay)
            loss_acc[...] += jnp.sum(terms, axis=0, keepdims=True)
            gate = jnp.where(margin >= 0.0, 1.0, decay) / (1.0 + decay)
            slope = (-LOGIT_SCALE / total_rows) * labels * gate
            across[block] += dot_nn(slope.astype(BF16), text)
            dots[...] += jnp.sum(slope * cosine, axis=0, keepdims=True)

        loop(0, blocks, tile)
        unit_txt = dot_nn(text, w_txt_ref[...])
        place = pl.ds(d * own, own)
        text_high[place], text_low[place] = split(-unit_txt * as_column(dots[...]))
        txt_turned[d] = text.T

    loop(0, SLOW, visit)
    d_high = query
    loop(0, 2 * fast - 1, lambda k: img_copy(my, mc, sibling, k).wait_send())

    def loss_along(d):
        return remote(loss_acc, loss_slow.at[mz], loss_sem.at[0, 0], loss_sem.at[0, 1], along(d))

    def loss_over(d):
        slot = loss_plane.at[mp]
        return remote(slot, slot, loss_sem.at[1, 0], loss_sem.at[1, 1], in_plane(d))

    for d in range(1, SLOW):
        loss_along(d).start()
    loss_slow[mz] = loss_acc[...]

    def turn(block):
        high, low = split(across[block])
        d_unit_img = dot_nn(high, w_txt_ref[...]) + dot_nn(low, w_txt_ref[...])
        unit_img = unit_high[block].astype(F32) + unit_low[block].astype(F32)
        d_proj_img = inv_all[block] * (
            d_unit_img - unit_img * jnp.sum(unit_img * d_unit_img, axis=1, keepdims=True)
        )
        d_high[block], low_part = split(d_proj_img)
        img_all[pl.ds(block * per, per), :, pl.ds(0, d_high.shape[2])] = low_part.reshape(per, own, -1)
        across_high[block], across_low[block] = high.T, low.T

    loop(0, blocks, turn)

    def core_copy(i):
        return remote(out_core.at[i], in_core.at[i], core_sem.at[0, i], core_sem.at[1, i], sibling)

    def fast_copy(i, d):
        return remote(
            out_fast.at[i, d - 1], in_fast.at[i, d - 1],
            fast_sem.at[0, i, d - 1], fast_sem.at[1, i, d - 1], across_fast(d),
        )

    def slow_copy(i):
        return remote(
            out_slow.at[i], in_slow.at[i], slow_sem.at[0, i], slow_sem.at[1, i], along(i + 1)
        )

    def make(i):
        first = pl.multiple_of(lax.rem(mz + 1 + i, SLOW) * LANES, LANES)
        columns = pl.ds(first, LANES)

        def add(block, sums):
            image, text = sums
            d_low = img_all[pl.ds(block * per, per), :, columns].reshape(size, LANES)
            image = image + dot_nn(img_turned[block], d_high[block, :, columns])
            image = image + dot_nn(img_turned[block], d_low)
            text = text + dot_nn(across_high[block], unit_high[block, :, columns])
            text = text + dot_nn(across_low[block], unit_high[block, :, columns])
            text = text + dot_nn(across_high[block], unit_low[block, :, columns])
            return image, text

        text = jnp.zeros((wide_txt, LANES), F32)
        for d in range(SLOW):
            place = pl.ds(d * own, own)
            text = text + dot_nn(txt_turned[d], text_high[place, columns])
            text = text + dot_nn(txt_turned[d], text_low[place, columns])
        sums = jnp.zeros((wide_img, LANES), F32), text
        sums = add(0, sums) if blocks == 1 else lax.fori_loop(0, blocks, add, sums)
        grads[i] = jnp.concatenate(sums).reshape(plane, part, LANES)

        def other(j):
            out_core[i, j] = pack(grads[i, (1 - mc) * fast + j], rows)

        loop(0, fast, other)
        core_copy(i).start()

    def summed(i, j):
        return grads[i, mc * fast + j] + unpack(in_core[i, j], part, rows)

    def pass_fast(i):
        core_copy(i).wait_recv()

        def one(d):
            out_fast[i, d - 1] = pack(summed(i, lax.rem(my + d, fast)), rows)
            fast_copy(i, d).start()

        loop(1, fast, one)

    def total(i):
        def one(d, value):
            fast_copy(i, d).wait_recv()
            return value + unpack(in_fast[i, d - 1], part, rows)

        return lax.fori_loop(1, fast, one, summed(i, my))

    def pass_slow(i):
        out_slow[i] = pack(total(i), rows)
        slow_copy(i).start()

    for i in range(SLOW + 2):
        if i < SLOW:
            make(i)
        if 1 <= i <= SLOW:
            pass_fast(i - 1)
        if 2 <= i <= SLOW:
            pass_slow(i - 2)

    remote(
        loss_slow.at[pl.ds(0, SLOW - 1)], loss_slow.at[pl.ds(0, SLOW - 1)],
        loss_sem.at[0, 0], loss_sem.at[0, 1], sibling,
    ).wait()
    loss_plane[mp] = jnp.sum(loss_slow[...], axis=0)
    loop(1, plane, lambda d: loss_over(d).start())

    value = total(SLOW - 1)
    for i in range(SLOW - 1):
        slow_copy(i).wait_recv()
        value = value + unpack(in_slow[i], part, rows)

    half = (rows + HEAD) // 32 * 16
    halves = [(0, half), (half, rows + HEAD - half)]

    def full_copy(h, z, y, c, dst, k):
        first, count = halves[h]
        slot = full_ref.at[(c * fast + y) * SLOW + z, pl.ds(first, count)]
        return remote(slot, slot, full_send.at[h, k], full_recv.at[h, device(z, y, c)], dst)

    full_ref[(mc * fast + my) * SLOW + mz] = pack(value, rows)
    base = SLOW - 1 + SLOW * (fast - 1)

    def forward(h, dz):
        z = lax.rem(mz + dz, SLOW)

        def one(d):
            k = SLOW - 1 + dz * (fast - 1) + d - 1
            full_copy(h, z, my, mc, across_fast(d), k).start()

        loop(1, fast, one)
        full_copy(h, z, my, mc, sibling, base + dz * fast).start()

    for h in range(2):
        for d in range(1, SLOW):
            full_copy(h, mz, my, mc, along(d), d - 1).start()
        forward(h, 0)
    for h in range(2):
        for dz in range(1, SLOW):
            full_copy(h, lax.rem(mz + dz, SLOW), my, mc, sibling, 0).wait_recv()
            forward(h, dz)

    for h in range(2):
        for dz in range(SLOW):
            z = lax.rem(mz + dz, SLOW)

            def one(d):
                y = lax.rem(my + d, fast)
                full_copy(h, z, y, mc, sibling, 0).wait_recv()
                full_copy(h, z, y, mc, sibling, base + dz * fast + d).start()

            loop(1, fast, one)

    remote(
        loss_plane.at[pl.ds(0, plane - 1)], loss_plane.at[pl.ds(0, plane - 1)],
        loss_sem.at[1, 0], loss_sem.at[1, 1], sibling,
    ).wait()
    loss_ref[...] = jnp.sum(jnp.sum(loss_plane[...], axis=0), axis=1, keepdims=True) / total_rows

    for h in range(2):
        for z in range(SLOW):
            loop(0, fast, lambda y: full_copy(h, z, y, 1 - mc, sibling, 0).wait_recv())
    for d in range(1, SLOW):
        txt_copy(mz, d).wait_send()
    for i in range(SLOW):
        core_copy(i).wait_send()
        loop(1, fast, lambda d: fast_copy(i, d).wait_send())
    for i in range(SLOW - 1):
        slow_copy(i).wait_send()
    for h in range(2):
        loop(0, n - 1, lambda k: full_copy(h, mz, my, mc, sibling, k).wait_send())


def body(n, image_feats, text_feats, class_ids, w_img, w_txt):
    own, wide_img = image_feats.shape
    wide_txt = text_feats.shape[1]
    shared = w_img.shape[1]
    fast = n // (2 * SLOW)
    plane = 2 * fast
    part = (wide_img + wide_txt) // plane
    rows = padded(part)
    tall = rows + HEAD
    size = min(plane, 4) * own
    blocks = plane * own // size
    columns = SLOW * own
    vmem = pltpu.VMEM
    dma = pltpu.SemaphoreType.DMA
    loss, full = pl.pallas_call(
        functools.partial(kernel, n),
        out_shape=(
            jax.ShapeDtypeStruct((1, 1), F32),
            jax.ShapeDtypeStruct((n, tall, LANES), jnp.int16),
        ),
        in_specs=[pl.BlockSpec(memory_space=pl.ANY)] * 5,
        out_specs=(pl.BlockSpec(memory_space=pltpu.VMEM),) * 2,
        scratch_shapes=[
            vmem(w_img.shape, BF16),
            vmem(w_txt.shape, BF16),
            vmem(text_feats.shape, BF16),
            vmem((plane, own, wide_img), BF16),
            vmem((SLOW, own, wide_txt), BF16),
            vmem((plane, 1, own), jnp.int32),
            vmem((SLOW, 1, own), jnp.int32),
            vmem((blocks, wide_img, size), BF16),
            vmem((blocks, wide_txt, size), BF16),
            vmem((blocks, wide_txt, size), BF16),
            vmem((blocks, size, shared), BF16),
            vmem((blocks, size, shared), BF16),
            vmem((blocks, size, 1), F32),
            vmem((blocks, size, wide_txt), BF16),
            vmem((blocks, size, wide_txt), F32),
            vmem((blocks, size, 1), F32),
            vmem((SLOW, wide_txt, own), BF16),
            vmem((columns, shared), BF16),
            vmem((columns, shared), BF16),
            vmem((1, own), F32),
            vmem((1, own), F32),
            vmem((SLOW, 1, own), F32),
            vmem((plane, 1, own), F32),
            vmem((SLOW, plane, part, LANES), F32),
            vmem((SLOW, fast, tall, LANES), jnp.int16),
            vmem((SLOW, fast, tall, LANES), jnp.int16),
            vmem((SLOW, fast - 1, tall, LANES), jnp.int16),
            vmem((SLOW, fast - 1, tall, LANES), jnp.int16),
            vmem((SLOW - 1, tall, LANES), jnp.int16),
            vmem((SLOW - 1, tall, LANES), jnp.int16),
            dma((6,)),
            dma((2 * fast - 1,)),
            dma((plane,)),
            dma((2, SLOW)),
            dma((4,)),
            dma((2, 2)),
            dma((2, SLOW)),
            dma((2, SLOW, fast - 1)),
            dma((2, SLOW - 1)),
            dma((2, n - 1)),
            dma((2, n)),
        ],
        compiler_params=pltpu.CompilerParams(
            collective_id=0, has_side_effects=True, vmem_limit_bytes=(40 if blocks == 1 else 60) * 2**20
        ),
    )(image_feats, text_feats, class_ids.reshape(1, own), w_img, w_txt)
    full = full.reshape(plane, SLOW, tall, LANES)
    scale = jnp.exp2(full[:, :, rows].astype(F32))
    grads = full[:, :, :part].astype(F32) * scale[:, :, None]
    grads = grads.transpose(0, 2, 1, 3).reshape(-1, shared)
    return loss.reshape(1), grads[:wide_img], grads[wide_img:]


def solution(mesh):
    return jax.shard_map(
        functools.partial(body, mesh.shape["blk"]),
        mesh=mesh,
        in_specs=(
            P(("groups", "blk"), None),
            P(("groups", "blk"), None),
            P(("groups", "blk")),
            P(),
            P(),
        ),
        out_specs=(P("groups"), P("groups", None), P("groups", None)),
        check_vma=False,
    )
```

```python
import functools

import jax
import jax.numpy as jnp
from jax import lax
from jax.experimental import pallas as pl
from jax.experimental.pallas import tpu as pltpu
from jax.sharding import PartitionSpec as P

LOGIT_SCALE = 10.0
LOGIT_BIAS = -10.0
NORM_EPS = 1e-06
F32 = jnp.float32
BF16 = jnp.bfloat16
LEVELS = 32767.0


LANES = 128
HEAD = 16
SLOW = 4


def padded(rows):
    return -(-rows // 16) * 16


def split(value):
    high = value.astype(BF16)
    return high, (value - high.astype(F32)).astype(BF16)


def pack(value, rows):
    peak = jnp.maximum(jnp.max(jnp.abs(value), axis=0, keepdims=True), 1e-30)
    power = jnp.ceil(jnp.log2(peak * (1.0001 / LEVELS)))
    levels = jnp.round(value * jnp.exp2(-power))
    parts = [levels]
    if rows > value.shape[0]:
        parts.append(jnp.zeros((rows - value.shape[0], LANES), F32))
    parts.append(jnp.broadcast_to(power, (HEAD, LANES)))
    return jnp.concatenate(parts).astype(jnp.int32).astype(jnp.int16)


def unpack(message, part, rows):
    wide = message.astype(jnp.int32).astype(F32)
    return wide[:part] * jnp.exp2(wide[rows:rows + 1])


def dot_nn(a, b):
    return jnp.dot(a, b, preferred_element_type=F32)


def dot_nt(a, b):
    return lax.dot_general(a, b, (((1,), (1,)), ((), ())), preferred_element_type=F32)


def dot_tn(a, b):
    return lax.dot_general(a, b, (((0,), (0,)), ((), ())), preferred_element_type=F32)


def as_column(row):
    length = row.shape[1]
    return jnp.broadcast_to(row, (length, length)).T[:, :1]


def loop(first, last, use):
    def step(i, carry):
        use(i)
        return carry

    lax.fori_loop(first, last, step, 0)


def kernel(
    n,
    img_hbm, txt_hbm, ids_hbm, w_img_hbm, w_txt_hbm,
    loss_ref, full_ref,
    w_img_ref, w_txt_ref, txt_ref, img_all, txt_all, ids_rows, ids_cols,
    img_turned, across_high, across_low, unit_high, unit_low, inv_all, query, across,
    row_ids, txt_turned, text_high, text_low, dots, loss_acc, loss_slow, loss_plane,
    grads, out_core, in_core, out_fast, in_fast, out_slow, in_slow,
    local_sem, img_send, img_recv, txt_sem, ids_sem, loss_sem,
    core_sem, fast_sem, slow_sem, full_send, full_recv,
):
    fast = n // (2 * SLOW)
    plane = 2 * fast
    own, wide_img = img_all.shape[1:]
    wide_txt = txt_all.shape[2]
    blocks, size = query.shape[:2]
    part = (wide_img + wide_txt) // plane
    rows = full_ref.shape[1] - HEAD
    per = size // own
    total_rows = n * own
    me = lax.axis_index("blk")
    mp = lax.rem(me, plane)
    mc = lax.rem(me, 2)
    my = mp // 2
    mz = me // plane

    def device(z, y, c):
        return (z * fast + y) * 2 + c

    def along(d):
        return device(lax.rem(mz + d, SLOW), my, mc)

    def across_fast(d):
        return device(mz, lax.rem(my + d, fast), mc)

    def in_plane(d):
        return mz * plane + lax.rem(mp + d, plane)

    sibling = device(mz, my, 1 - mc)

    barrier = pltpu.get_barrier_semaphore()
    for d in range(1, SLOW):
        pl.semaphore_signal(barrier, inc=1, device_id={"blk": along(d)})
    loop(1, plane, lambda d: pl.semaphore_signal(barrier, inc=1, device_id={"blk": in_plane(d)}))

    loads = [
        pltpu.make_async_copy(a, b, local_sem.at[k])
        for k, (a, b) in enumerate([
            (txt_hbm, txt_ref), (w_txt_hbm, w_txt_ref), (img_hbm, img_all.at[mp]),
            (w_img_hbm, w_img_ref), (ids_hbm, ids_rows.at[mp]), (ids_hbm, ids_cols.at[mz]),
        ])
    ]
    for load in loads:
        load.start()

    def remote(src, dst, send, recv, where):
        return pltpu.make_async_remote_copy(
            src_ref=src, dst_ref=dst, send_sem=send, recv_sem=recv, device_id={"blk": where}
        )

    def img_copy(y, c, dst, k):
        slot = img_all.at[y * 2 + c]
        return remote(slot, slot, img_send.at[k], img_recv.at[y * 2 + c], dst)

    def txt_copy(z, d):
        return remote(txt_all.at[z], txt_all.at[z], txt_sem.at[0, d], txt_sem.at[1, z], along(d))

    def ids_row_copy(d):
        slot = ids_rows.at[mp]
        return remote(slot, slot, ids_sem.at[0], ids_sem.at[1], in_plane(d))

    def ids_col_copy(d):
        slot = ids_cols.at[mz]
        return remote(slot, slot, ids_sem.at[2], ids_sem.at[3], along(d))

    loads[0].wait()
    loads[1].wait()
    proj_txt = dot_nn(txt_ref[...], w_txt_ref[...])
    inv_txt = lax.rsqrt(jnp.sum(proj_txt * proj_txt, axis=1, keepdims=True) + NORM_EPS)
    txt_all[mz] = (txt_ref[...].astype(F32) * inv_txt).astype(BF16)
    for load in loads[2:]:
        load.wait()
    pl.semaphore_wait(barrier, SLOW + plane - 2)

    for d in range(1, SLOW):
        txt_copy(mz, d).start()
    loop(1, fast, lambda d: img_copy(my, mc, across_fast(d), d).start())
    img_copy(my, mc, sibling, 0).start()
    for d in range(1, SLOW):
        ids_col_copy(d).start()
    loop(1, plane, lambda d: ids_row_copy(d).start())

    loss_acc[...] = jnp.zeros_like(loss_acc)

    def pass_on(d):
        y = lax.rem(my + d, fast)
        img_copy(y, mc, sibling, 0).wait_recv()
        img_copy(y, mc, sibling, fast - 1 + d).start()

    loop(1, fast, pass_on)
    loop(0, fast, lambda d: img_copy(d, 1 - mc, sibling, 0).wait_recv())
    remote(
        ids_rows.at[pl.ds(0, plane - 1)], ids_rows.at[pl.ds(0, plane - 1)],
        ids_sem.at[0], ids_sem.at[1], sibling,
    ).wait()

    def project(block):
        img = img_all[pl.ds(block * per, per)].reshape(size, wide_img)
        proj_img = dot_nn(img, w_img_ref[...])
        inv_img = lax.rsqrt(jnp.sum(proj_img * proj_img, axis=1, keepdims=True) + NORM_EPS)
        unit_img = proj_img * inv_img
        high, low = split(unit_img)
        query[block] = (dot_nt(high, w_txt_ref[...]) + dot_nt(low, w_txt_ref[...])).astype(BF16)
        unit_high[block], unit_low[block] = high, low
        inv_all[block] = inv_img
        img_turned[block] = img.T
        across[block] = jnp.zeros((size, wide_txt), F32)
        row_ids[block] = jnp.concatenate(
            [as_column(ids_rows[block * per + i].astype(F32)) for i in range(per)]
        )

    loop(0, blocks, project)
    remote(
        ids_cols.at[pl.ds(0, SLOW - 1)], ids_cols.at[pl.ds(0, SLOW - 1)],
        ids_sem.at[2], ids_sem.at[3], sibling,
    ).wait()

    def visit(d):
        z = lax.rem(mz + d, SLOW)

        @pl.when(d > 0)
        def _():
            txt_copy(z, 0).wait_recv()

        text = txt_all[z]
        ids = ids_cols[z].astype(F32)
        dots[...] = jnp.zeros_like(dots)

        def tile(block):
            cosine = dot_nt(query[block], text)
            logits = LOGIT_SCALE * cosine + LOGIT_BIAS
            labels = jnp.where(row_ids[block] == ids, 1.0, -1.0).astype(F32)
            margin = -labels * logits
            decay = jnp.exp(-jnp.abs(margin))
            terms = jnp.maximum(margin, 0.0) + jnp.log1p(decay)
            loss_acc[...] += jnp.sum(terms, axis=0, keepdims=True)
            gate = jnp.where(margin >= 0.0, 1.0, decay) / (1.0 + decay)
            slope = (-LOGIT_SCALE / total_rows) * labels * gate
            across[block] += dot_nn(slope.astype(BF16), text)
            dots[...] += jnp.sum(slope * cosine, axis=0, keepdims=True)

        loop(0, blocks, tile)
        unit_txt = dot_nn(text, w_txt_ref[...])
        place = pl.ds(d * own, own)
        text_high[place], text_low[place] = split(-unit_txt * as_column(dots[...]))
        txt_turned[d] = text.T

    loop(0, SLOW, visit)
    d_high = query
    loop(0, 2 * fast - 1, lambda k: img_copy(my, mc, sibling, k).wait_send())

    def loss_along(d):
        return remote(loss_acc, loss_slow.at[mz], loss_sem.at[0, 0], loss_sem.at[0, 1], along(d))

    def loss_over(d):
        slot = loss_plane.at[mp]
        return remote(slot, slot, loss_sem.at[1, 0], loss_sem.at[1, 1], in_plane(d))

    for d in range(1, SLOW):
        loss_along(d).start()
    loss_slow[mz] = loss_acc[...]

    def turn(block):
        high, low = split(across[block])
        d_unit_img = dot_nn(high, w_txt_ref[...]) + dot_nn(low, w_txt_ref[...])
        unit_img = unit_high[block].astype(F32) + unit_low[block].astype(F32)
        d_proj_img = inv_all[block] * (
            d_unit_img - unit_img * jnp.sum(unit_img * d_unit_img, axis=1, keepdims=True)
        )
        d_high[block], low_part = split(d_proj_img)
        img_all[pl.ds(block * per, per), :, pl.ds(0, d_high.shape[2])] = low_part.reshape(per, own, -1)
        across_high[block], across_low[block] = high.T, low.T

    loop(0, blocks, turn)

    def core_copy(i):
        return remote(out_core.at[i], in_core.at[i], core_sem.at[0, i], core_sem.at[1, i], sibling)

    def fast_copy(i, d):
        return remote(
            out_fast.at[i, d - 1], in_fast.at[i, d - 1],
            fast_sem.at[0, i, d - 1], fast_sem.at[1, i, d - 1], across_fast(d),
        )

    def slow_copy(i):
        return remote(
            out_slow.at[i], in_slow.at[i], slow_sem.at[0, i], slow_sem.at[1, i], along(i + 1)
        )

    def make(i):
        first = pl.multiple_of(lax.rem(mz + 1 + i, SLOW) * LANES, LANES)
        columns = pl.ds(first, LANES)

        def add(block, sums):
            image, text = sums
            d_low = img_all[pl.ds(block * per, per), :, columns].reshape(size, LANES)
            image = image + dot_nn(img_turned[block], d_high[block, :, columns])
            image = image + dot_nn(img_turned[block], d_low)
            text = text + dot_nn(across_high[block], unit_high[block, :, columns])
            text = text + dot_nn(across_low[block], unit_high[block, :, columns])
            text = text + dot_nn(across_high[block], unit_low[block, :, columns])
            return image, text

        text = jnp.zeros((wide_txt, LANES), F32)
        for d in range(SLOW):
            place = pl.ds(d * own, own)
            text = text + dot_nn(txt_turned[d], text_high[place, columns])
            text = text + dot_nn(txt_turned[d], text_low[place, columns])
        sums = jnp.zeros((wide_img, LANES), F32), text
        sums = add(0, sums) if blocks == 1 else lax.fori_loop(0, blocks, add, sums)
        grads[i] = jnp.concatenate(sums).reshape(plane, part, LANES)

        def other(j):
            out_core[i, j] = pack(grads[i, (1 - mc) * fast + j], rows)

        loop(0, fast, other)
        core_copy(i).start()

    def summed(i, j):
        return grads[i, mc * fast + j] + unpack(in_core[i, j], part, rows)

    def pass_fast(i):
        core_copy(i).wait_recv()

        def one(d):
            out_fast[i, d - 1] = pack(summed(i, lax.rem(my + d, fast)), rows)
            fast_copy(i, d).start()

        loop(1, fast, one)

    def total(i):
        def one(d, value):
            fast_copy(i, d).wait_recv()
            return value + unpack(in_fast[i, d - 1], part, rows)

        return lax.fori_loop(1, fast, one, summed(i, my))

    def pass_slow(i):
        out_slow[i] = pack(total(i), rows)
        slow_copy(i).start()

    for i in range(SLOW + 2):
        if i < SLOW:
            make(i)
        if 1 <= i <= SLOW:
            pass_fast(i - 1)
        if 2 <= i <= SLOW:
            pass_slow(i - 2)

    remote(
        loss_slow.at[pl.ds(0, SLOW - 1)], loss_slow.at[pl.ds(0, SLOW - 1)],
        loss_sem.at[0, 0], loss_sem.at[0, 1], sibling,
    ).wait()
    loss_plane[mp] = jnp.sum(loss_slow[...], axis=0)
    loop(1, plane, lambda d: loss_over(d).start())

    value = total(SLOW - 1)
    for i in range(SLOW - 1):
        slow_copy(i).wait_recv()
        value = value + unpack(in_slow[i], part, rows)

    half = (rows + HEAD) // 32 * 16
    halves = [(0, half), (half, rows + HEAD - half)]

    def full_copy(h, z, y, c, dst, k):
        first, count = halves[h]
        slot = full_ref.at[(c * fast + y) * SLOW + z, pl.ds(first, count)]
        return remote(slot, slot, full_send.at[h, k], full_recv.at[h, device(z, y, c)], dst)

    full_ref[(mc * fast + my) * SLOW + mz] = pack(value, rows)
    base = SLOW - 1 + SLOW * (fast - 1)

    def forward(h, dz):
        z = lax.rem(mz + dz, SLOW)

        def one(d):
            k = SLOW - 1 + dz * (fast - 1) + d - 1
            full_copy(h, z, my, mc, across_fast(d), k).start()

        loop(1, fast, one)
        full_copy(h, z, my, mc, sibling, base + dz * fast).start()

    for h in range(2):
        for d in range(1, SLOW):
            full_copy(h, mz, my, mc, along(d), d - 1).start()
        forward(h, 0)
    for h in range(2):
        for dz in range(1, SLOW):
            full_copy(h, lax.rem(mz + dz, SLOW), my, mc, sibling, 0).wait_recv()
            forward(h, dz)

    for h in range(2):
        for dz in range(SLOW):
            z = lax.rem(mz + dz, SLOW)

            def one(d):
                y = lax.rem(my + d, fast)
                full_copy(h, z, y, mc, sibling, 0).wait_recv()
                full_copy(h, z, y, mc, sibling, base + dz * fast + d).start()

            loop(1, fast, one)

    remote(
        loss_plane.at[pl.ds(0, plane - 1)], loss_plane.at[pl.ds(0, plane - 1)],
        loss_sem.at[1, 0], loss_sem.at[1, 1], sibling,
    ).wait()
    loss_ref[...] = jnp.sum(jnp.sum(loss_plane[...], axis=0), axis=1, keepdims=True) / total_rows

    for h in range(2):
        for z in range(SLOW):
            loop(0, fast, lambda y: full_copy(h, z, y, 1 - mc, sibling, 0).wait_recv())
    for d in range(1, SLOW):
        txt_copy(mz, d).wait_send()
    for i in range(SLOW):
        core_copy(i).wait_send()
        loop(1, fast, lambda d: fast_copy(i, d).wait_send())
    for i in range(SLOW - 1):
        slow_copy(i).wait_send()
    for h in range(2):
        loop(0, n - 1, lambda k: full_copy(h, mz, my, mc, sibling, k).wait_send())


def body(n, image_feats, text_feats, class_ids, w_img, w_txt):
    own, wide_img = image_feats.shape
    wide_txt = text_feats.shape[1]
    shared = w_img.shape[1]
    fast = n // (2 * SLOW)
    plane = 2 * fast
    part = (wide_img + wide_txt) // plane
    rows = padded(part)
    tall = rows + HEAD
    size = min(plane, 4) * own
    blocks = plane * own // size
    columns = SLOW * own
    vmem = pltpu.VMEM
    dma = pltpu.SemaphoreType.DMA
    loss, full = pl.pallas_call(
        functools.partial(kernel, n),
        out_shape=(
            jax.ShapeDtypeStruct((1, 1), F32),
            jax.ShapeDtypeStruct((n, tall, LANES), jnp.int16),
        ),
        in_specs=[pl.BlockSpec(memory_space=pl.ANY)] * 5,
        out_specs=(pl.BlockSpec(memory_space=pltpu.VMEM),) * 2,
        scratch_shapes=[
            vmem(w_img.shape, BF16),
            vmem(w_txt.shape, BF16),
            vmem(text_feats.shape, BF16),
            vmem((plane, own, wide_img), BF16),
            vmem((SLOW, own, wide_txt), BF16),
            vmem((plane, 1, own), jnp.int32),
            vmem((SLOW, 1, own), jnp.int32),
            vmem((blocks, wide_img, size), BF16),
            vmem((blocks, wide_txt, size), BF16),
            vmem((blocks, wide_txt, size), BF16),
            vmem((blocks, size, shared), BF16),
            vmem((blocks, size, shared), BF16),
            vmem((blocks, size, 1), F32),
            vmem((blocks, size, wide_txt), BF16),
            vmem((blocks, size, wide_txt), F32),
            vmem((blocks, size, 1), F32),
            vmem((SLOW, wide_txt, own), BF16),
            vmem((columns, shared), BF16),
            vmem((columns, shared), BF16),
            vmem((1, own), F32),
            vmem((1, own), F32),
            vmem((SLOW, 1, own), F32),
            vmem((plane, 1, own), F32),
            vmem((SLOW, plane, part, LANES), F32),
            vmem((SLOW, fast, tall, LANES), jnp.int16),
            vmem((SLOW, fast, tall, LANES), jnp.int16),
            vmem((SLOW, fast - 1, tall, LANES), jnp.int16),
            vmem((SLOW, fast - 1, tall, LANES), jnp.int16),
            vmem((SLOW - 1, tall, LANES), jnp.int16),
            vmem((SLOW - 1, tall, LANES), jnp.int16),
            dma((6,)),
            dma((2 * fast - 1,)),
            dma((plane,)),
            dma((2, SLOW)),
            dma((4,)),
            dma((2, 2)),
            dma((2, SLOW)),
            dma((2, SLOW, fast - 1)),
            dma((2, SLOW - 1)),
            dma((2, n - 1)),
            dma((2, n)),
        ],
        compiler_params=pltpu.CompilerParams(
            collective_id=0, has_side_effects=True, vmem_limit_bytes=(63 if blocks == 1 else 60) * 2**20
        ),
    )(image_feats, text_feats, class_ids.reshape(1, own), w_img, w_txt)
    full = full.reshape(plane, SLOW, tall, LANES)
    scale = jnp.exp2(full[:, :, rows].astype(F32))
    grads = full[:, :, :part].astype(F32) * scale[:, :, None]
    grads = grads.transpose(0, 2, 1, 3).reshape(-1, shared)
    return loss.reshape(1), grads[:wide_img], grads[wide_img:]


def solution(mesh):
    return jax.shard_map(
        functools.partial(body, mesh.shape["blk"]),
        mesh=mesh,
        in_specs=(
            P(("groups", "blk"), None),
            P(("groups", "blk"), None),
            P(("groups", "blk")),
            P(),
            P(),
        ),
        out_specs=(P("groups"), P("groups", None), P("groups", None)),
        check_vma=False,
    )
```
